32 devices in a mesh: groups: 2 (over y), mesh: 4 (over z), grid: 2 (over x), mp: 2 (over core).
Axes of the slice: x: 2, y: 2, z: 4, core: 2. Of those that a mesh axis runs over, the one named last changes fastest.
Arguments:
- grid_latent: bfloat16 [4096, 512], P(('groups', 'mesh', 'grid'), 'mp'), parts along dimension 0, may hold values from -6 to 6
- mesh_latent: bfloat16 [8192, 512], P(('groups', 'mesh', 'grid'), 'mp'), parts along dimension 0, may hold values from -6 to 6
- local_targets: int32 [2048, 3], P(('mesh', 'grid')), may hold values from 0 to 511
- grid_slots: int32 [32, 32], P(('mesh', 'grid')), may hold values from 0 to 255
- mesh_slots: int32 [32, 32], P(('mesh', 'grid')), may hold values from -1 to 511, as said below
- mesh_links: int32 [4096, 6], P(('mesh', 'grid')), may hold values from 0 to 1535
- encode_in: bfloat16 [512, 512], P(None, 'mp'), may hold values from -0.25 to 0.25
- encode_out: bfloat16 [512, 512], P('mp'), may hold values from -0.25 to 0.25
- process_in: bfloat16 [512, 512], P(None, 'mp'), may hold values from -0.25 to 0.25
- process_out: bfloat16 [512, 512], P('mp'), may hold values from -0.25 to 0.25
- decode_in: bfloat16 [512, 512], P(None, 'mp'), may hold values from -0.25 to 0.25
- decode_out: bfloat16 [512, 512], P('mp'), may hold values from -0.25 to 0.25
- cotangent: bfloat16 [4096, 512], P(('groups', 'mesh', 'grid'), 'mp'), parts along dimension 0, may hold values from -0.0625 to 0.0625
Outputs:
- prediction: bfloat16 [4096, 512], P(('groups', 'mesh', 'grid'), 'mp'), parts along dimension 0
- grad_up: float32 [1024, 512], P('groups', 'mp'), parts along dimension 0
- grad_down: float32 [1024, 512], P(('groups', 'mp')), parts along dimension 0
The draws below stay inside these ranges and needn't reach their ends.
There are 2 independent parts, one for each index of `groups`. The reference program is written for one: setup_inputs(seed, part) draws one part's arguments, and reference() takes and returns one part's arrays. A program takes and returns all parts, laid end to end along the dimension named above; an argument that names none is the same for every part. Nothing has to cross between parts.
Inputs may be any that keep to these rules, and one draw needn't show every extreme that they name: `mesh_slots`: within each row the slots in use come first, 16 of them or more; one partition receives all 32 slots from each of its four nearest partitions.
All inputs are finite; a program needn't handle non-finite values.
Results may differ from the reference program's by a relative error of at most 0.0085.
Values may be sent and summed in bfloat16 or wider, within the bound.
A program may use at most 64 MiB of HBM per device.

```python
import jax
import jax.numpy as jnp
from jax import lax

L = 512
G_DEV = 256
M_DEV = 512
LOCAL = 3
LINKS = 6
SECTIONS = 8
CAP = 32
GRID = 2048
MESH = 4096


def draw_mesh_slots(key, part):
    key = jax.random.fold_in(key, 11)
    key_fullest, key_count, key_target = jax.random.split(key, 3)
    fullest = jax.random.randint(key_fullest, (), 0, SECTIONS)
    receiver = jnp.arange(SECTIONS, dtype=jnp.int32)
    in_use = jax.random.randint(key_count, (SECTIONS, 4), CAP // 2, CAP + 1)
    in_use = jnp.where(receiver[:, None] == fullest, CAP, in_use)
    targets = jax.random.randint(key_target, (SECTIONS, 4, CAP), 0, M_DEV)
    position = jnp.arange(CAP, dtype=jnp.int32)
    chosen = jnp.where(position[None, None, :] < in_use[:, :, None], targets, -1)
    return chosen.reshape(SECTIONS * 4, CAP).astype(jnp.int32)


def set_ends(drawn, rng, smallest, top_value):
    longest = drawn.shape.index(max(drawn.shape))
    spots = []
    for shift in (0, 1):
        where = [jax.random.randint(jax.random.fold_in(rng, axis), (), 0, length) for axis, length in enumerate(drawn.shape)]
        where[longest] = (where[longest] + shift) % drawn.shape[longest]
        spots.append(tuple(where))
    return drawn.at[spots[0]].set(smallest).at[spots[1]].set(top_value)


def shard_levels(own_key, extent, shards, least, largest):
    level, own = 1.0, jax.random.fold_in(own_key, 6)
    for axis_at, blocks in shards:
        steps = jnp.exp(jax.random.uniform(jax.random.fold_in(own, axis_at), (blocks,), jnp.float32, least / len(shards), largest / len(shards)))
        level = level * jnp.repeat(steps, extent[axis_at] // blocks).reshape([-1 if axis == axis_at else 1 for axis in range(len(extent))])
    return level


def normal_values(stream_key, shape, scale, bound, cuts=(), held_as=jnp.bfloat16):
    values = scale * jax.random.normal(stream_key, shape, jnp.float32)
    if cuts:
        values = values * shard_levels(stream_key, shape, cuts, -0.22, 0.18)
    return jnp.clip(values, -bound, bound).astype(held_as)


def setup_inputs(seed: int = 0, part: int = 0) -> dict:
    seeds = jax.random.split(jax.random.key(seed), 14)
    part_keys = jax.random.split(jax.random.fold_in(seeds[13], part), 14)
    grid_latent = normal_values(part_keys[0], (GRID, L), 1.0, 6.0, ((0, 8), (1, 2)))
    mesh_latent = normal_values(part_keys[1], (MESH, L), 1.0, 6.0, ((0, 8), (1, 2)))
    local_targets = set_ends(jax.random.randint(seeds[2], (GRID, LOCAL), 0, M_DEV), jax.random.fold_in(seeds[2], 1), 0, M_DEV - 1).astype(jnp.int32)
    grid_slots = set_ends(jax.random.randint(seeds[3], (4 * SECTIONS, CAP), 0, G_DEV), jax.random.fold_in(seeds[3], 1), 0, G_DEV - 1).astype(jnp.int32)
    mesh_slots = draw_mesh_slots(jax.random.fold_in(seeds[13], 71), part)
    mesh_links = set_ends(jax.random.randint(seeds[5], (MESH, LINKS), 0, 3 * M_DEV), jax.random.fold_in(seeds[5], 1), 0, (3 * M_DEV) - 1).astype(jnp.int32)
    encode_in = normal_values(seeds[6], (L, L), L ** -0.5, 0.25, ((1, 2),))
    encode_out = normal_values(seeds[7], (L, L), L ** -0.5, 0.25, ((0, 2),))
    process_in = normal_values(seeds[8], (L, L), L ** -0.5, 0.25, ((1, 2),))
    process_out = normal_values(seeds[9], (L, L), L ** -0.5, 0.25, ((0, 2),))
    decode_in = normal_values(seeds[10], (L, L), L ** -0.5, 0.25, ((1, 2),))
    decode_out = normal_values(seeds[11], (L, L), L ** -0.5, 0.25, ((0, 2),))
    cotangent = normal_values(part_keys[12], (GRID, L), 0.01, 0.0625, ((0, 8), (1, 2)))
    return {"grid_latent": grid_latent, "mesh_latent": mesh_latent, "local_targets": local_targets, "grid_slots": grid_slots, "mesh_slots": mesh_slots, "mesh_links": mesh_links, "encode_in": encode_in, "encode_out": encode_out, "process_in": process_in, "process_out": process_out, "decode_in": decode_in, "decode_out": decode_out, "cotangent": cotangent}


def mlp_block(values, weight_in, weight_out):
    stored = lax.optimization_barrier(values.astype(jnp.bfloat16)).astype(jnp.float32)
    center = stored - lax.optimization_barrier(jnp.mean(stored, axis=-1, keepdims=True))
    spread = lax.optimization_barrier(jnp.mean(center * center, axis=-1, keepdims=True))
    normed = (center * lax.rsqrt(spread + 1e-05)).astype(jnp.bfloat16)
    before = jnp.dot(normed, weight_in, preferred_element_type=jnp.float32)
    activated = jax.nn.silu(before).astype(jnp.bfloat16)
    return (jnp.dot(activated, weight_out, preferred_element_type=jnp.float32), normed, before, activated)

def remote_edges(grid_slots, mesh_slots):
    offsets = jnp.array([-2, -1, 1, 2], dtype=jnp.int32)
    receiving = jnp.arange(SECTIONS, dtype=jnp.int32)[:, None, None]
    which = jnp.arange(4, dtype=jnp.int32)[None, :, None]
    column = jnp.arange(CAP, dtype=jnp.int32)[None, None, :]
    sending = (receiving - offsets[None, :, None]) % SECTIONS
    slot_table = grid_slots.reshape(SECTIONS, 4, CAP)
    slot_rows = slot_table[sending, which, column]
    slot_targets = mesh_slots.reshape(SECTIONS, 4, CAP)
    in_use = (slot_targets >= 0).reshape(-1)
    source = (sending * G_DEV + slot_rows).reshape(-1).astype(jnp.int32)
    target = (receiving * M_DEV + jnp.maximum(slot_targets, 0)).reshape(-1).astype(jnp.int32)
    return (source, target, in_use)

def reference(grid_latent, mesh_latent, local_targets, grid_slots, mesh_slots, mesh_links, encode_in, encode_out, process_in, process_out, decode_in, decode_out, cotangent):
    source, target, in_use = remote_edges(grid_slots, mesh_slots)
    usable = in_use[:, None]
    grid_index = jnp.arange(GRID, dtype=jnp.int32)
    local_base = grid_index // G_DEV * M_DEV
    grid_values = grid_latent.astype(jnp.float32)
    moved = jnp.where(usable, grid_values[source], 0.0)
    mesh_sum = jax.ops.segment_sum(moved, target, num_segments=MESH)
    for column in range(LOCAL):
        local_to = (local_base + local_targets[:, column].astype(jnp.int32)).astype(jnp.int32)
        mesh_sum = mesh_sum + jax.ops.segment_sum(grid_values, local_to, num_segments=MESH)
    encoded = mlp_block(mesh_sum, encode_in, encode_out)[0]
    mesh_state = (mesh_latent.astype(jnp.float32) + encoded).astype(jnp.bfloat16)
    node_index = jnp.arange(MESH, dtype=jnp.int32)
    section = node_index // M_DEV
    gathered = jnp.zeros((MESH, L), jnp.float32)
    for column in range(LINKS):
        chosen = mesh_links[:, column].astype(jnp.int32)
        anchor = (section - 1 + chosen // M_DEV) % SECTIONS * M_DEV + chosen % M_DEV
        gathered = gathered + mesh_state[anchor].astype(jnp.float32)
    processed = mlp_block(gathered, process_in, process_out)[0]
    mesh_final = (mesh_state.astype(jnp.float32) + processed).astype(jnp.bfloat16)
    final_values = mesh_final.astype(jnp.float32)
    returned = jnp.where(usable, final_values[target], 0.0)
    grid_sum = jax.ops.segment_sum(returned, source, num_segments=GRID)
    for column in range(LOCAL):
        local_to = (local_base + local_targets[:, column].astype(jnp.int32)).astype(jnp.int32)
        grid_sum = grid_sum + final_values[local_to]
    decoded, normed, before, activated = mlp_block(grid_sum, decode_in, decode_out)
    prediction = (grid_latent.astype(jnp.float32) + decoded).astype(jnp.bfloat16)
    grad_down = jnp.dot(activated.T, cotangent, preferred_element_type=jnp.float32)
    hidden_grad = jnp.dot(cotangent, decode_out.T, preferred_element_type=jnp.float32)
    gate_value = jax.nn.sigmoid(before)
    before_grad = (hidden_grad * gate_value * (1.0 + before * (1.0 - gate_value))).astype(jnp.bfloat16)
    grad_up = jnp.dot(normed.T, before_grad, preferred_element_type=jnp.float32)
    return (prediction, grad_up, grad_down)
```

```python
import functools

import jax
import jax.numpy as jnp
from jax import lax
from jax.experimental import pallas as pl
from jax.experimental.pallas import tpu as pltpu
from jax.sharding import PartitionSpec as P

MESH = pl.DeviceIdType.MESH
slot_offsets = (-2, -1, 1, 2)
FIRST = (((0,), (0,)), ((), ()))
SECOND = (((1,), (1,)), ((), ()))
LANES = 128


def mm(a, b, dims=(((1,), (0,)), ((), ()))):
    return lax.dot_general(a, b, dims, preferred_element_type=jnp.float32)


def plan(mesh_axis, grid_axis, width, hidden):
    devices = mesh_axis * grid_axis
    total = 2 * width * hidden // LANES
    pieces = max(1, min(4, total // (16 * devices)))
    piece = total // pieces
    by_grid = piece // grid_axis
    return total, pieces, piece, by_grid, by_grid // mesh_axis


def kernel(
    sizes,
    grid_ref,
    mesh_ref,
    targets_ref,
    gslots_ref,
    mslots_ref,
    links_ref,
    ein_ref,
    eout_ref,
    pin_ref,
    pout_ref,
    din_ref,
    dout_ref,
    cot_ref,
    pred_ref,
    red_ref,
    counts,
    local_t,
    picker_t,
    placer,
    out_slots,
    in_slots,
    back_out,
    back_in,
    acc,
    own,
    other,
    part_out,
    part_in,
    keep,
    state,
    before_halo,
    after_halo,
    final,
    gown,
    gother,
    gpart_out,
    gpart_in,
    cot_other,
    hidden_grad,
    grads,
    stage,
    rx,
    acc_x,
    stage_z,
    rz,
    send_sems,
    recv_sems,
):
    mesh_n, grid_n = sizes
    devices = mesh_n * grid_n
    grid_rows, half = grid_ref.shape
    mesh_rows = mesh_ref.shape[0]
    hidden = ein_ref.shape[1]
    width = ein_ref.shape[0]
    cap = gslots_ref.shape[1] // 4
    total, pieces, piece, by_grid, by_mesh = plan(mesh_n, grid_n, width, hidden)
    mz, mx, mp = (lax.axis_index("mesh"), lax.axis_index("grid"), lax.axis_index("mp"))
    place = mz * grid_n + mx
    peer = {"mp": 1 - mp}

    def at(offset):
        spot = lax.rem(place + (devices + offset), devices)
        return {"mesh": lax.div(spot, grid_n), "grid": lax.rem(spot, grid_n)}

    def along(axis, me, count, step):
        return {axis: lax.rem(me + step, count)}

    started = []

    def send(src, dst, device):
        index = len(started)
        copy = pltpu.make_async_remote_copy(
            src_ref=src,
            dst_ref=dst,
            send_sem=send_sems.at[index],
            recv_sem=recv_sems.at[index],
            device_id=device,
            device_id_type=MESH,
        )
        copy.start()
        started.append(copy)
        return copy

    partners = [peer] + [at(o) for o in slot_offsets]
    partners += [along("grid", mx, grid_n, d) for d in range(1, grid_n)]
    partners += [along("mesh", mz, mesh_n, d) for d in range(1, mesh_n)]
    barrier = pltpu.get_barrier_semaphore()
    for device in partners:
        pl.semaphore_signal(barrier, inc=1, device_id=device, device_id_type=MESH)

    rows_at = lambda n, m: lax.broadcasted_iota(jnp.int32, (n, m), 0)
    picker_t[...] = (
        (rows_at(grid_rows, 4 * cap) == gslots_ref[...]).astype(jnp.float32).astype(jnp.bfloat16)
    )
    placer[...] = (
        (rows_at(mesh_rows, 4 * cap) == mslots_ref[...]).astype(jnp.float32).astype(jnp.bfloat16)
    )
    out_slots[...] = mm(picker_t[...], grid_ref[...], FIRST).astype(jnp.bfloat16)
    pl.semaphore_wait(barrier, len(partners))

    slots = []
    for k, offset in enumerate(slot_offsets):
        rows = pl.ds(k * cap, cap)
        slots.append(send(out_slots.at[rows], in_slots.at[rows], at(offset)))
    cot_copy = send(cot_ref, cot_other, peer)

    def count_into(dst, src_ref, block):
        rows, span = dst.shape
        columns = src_ref.shape[1]

        def body(i, carry):
            here = pl.ds(pl.multiple_of(i * block, block), block)
            window = lax.broadcasted_iota(jnp.int32, (block, span), 1)
            links = src_ref[here, :]
            found = jnp.zeros((block, span), jnp.float32)
            for k in range(columns):
                found = found + (links[:, k : k + 1] == window).astype(jnp.float32)
            dst[here, :] = found.astype(jnp.bfloat16)
            return carry

        lax.fori_loop(0, rows // block, body, 0)

    count_into(local_t, targets_ref, 32)
    chunk = 256
    chunks = mesh_rows // chunk
    chunk_rows = [pl.ds(c * chunk, chunk) for c in range(chunks)]
    for rows in chunk_rows:
        acc[rows, :] = mm(local_t[:, rows], grid_ref[...], FIRST)

    first = pl.ds(pl.multiple_of(mp * half, half), half)
    second = pl.ds(pl.multiple_of((1 - mp) * half, half), half)

    def normalise(mine, theirs):
        a, b = (mine.astype(jnp.float32), theirs.astype(jnp.float32))
        mean = (jnp.sum(a, axis=1, keepdims=True) + jnp.sum(b, axis=1, keepdims=True)) / width
        a, b = (a - mean, b - mean)
        spread = jnp.sum(a * a, axis=1, keepdims=True) + jnp.sum(b * b, axis=1, keepdims=True)
        scale = lax.rsqrt(spread / width + 1e-05)
        return ((a * scale).astype(jnp.bfloat16), (b * scale).astype(jnp.bfloat16))

    def hidden_units(mine, theirs, in_ref):
        na, nb = normalise(mine, theirs)
        return (na, nb, mm(na, in_ref[first, :]) + mm(nb, in_ref[second, :]))

    def widen(which, rows):
        return send(own.at[which, rows], other.at[which, rows], peer)

    def mesh_block(which, wide, in_ref, out_ref, base_ref, dst_ref, after):
        parts = []
        for rows, copy in zip(chunk_rows, wide):
            copy.wait_recv()
            before = hidden_units(own[which, rows, :], other[which, rows, :], in_ref)[2]
            activated = (before * jax.nn.sigmoid(before)).astype(jnp.bfloat16)
            part_out[which, rows, :] = mm(activated, out_ref[:, second]).astype(jnp.bfloat16)
            parts.append(send(part_out.at[which, rows], part_in.at[which, rows], peer))
            keep[rows, :] = mm(activated, out_ref[:, first]) + base_ref[rows, :].astype(jnp.float32)
        for rows, copy in zip(chunk_rows, parts):
            copy.wait_recv()
            dst_ref[rows, :] = (
                keep[rows, :] + part_in[which, rows, :].astype(jnp.float32)
            ).astype(jnp.bfloat16)
            after(rows)

    for copy in slots:
        copy.wait_recv()
    wide = []
    for rows in chunk_rows:
        own[0, rows, :] = (mm(placer[rows, :], in_slots[...]) + acc[rows, :]).astype(jnp.bfloat16)
        wide.append(widen(0, rows))

    count_into(counts, links_ref, 32)
    halo = []

    def send_halo(rows):
        halo.append(send(state.at[rows], before_halo.at[rows], at(1)))
        halo.append(send(state.at[rows], after_halo.at[rows], at(-1)))

    mesh_block(0, wide, ein_ref, eout_ref, mesh_ref, state, send_halo)

    cot_copy.wait_recv()
    hidden_grad[...] = mm(cot_ref[...], dout_ref[:, first], SECOND) + mm(
        cot_other[...], dout_ref[:, second], SECOND
    )
    for rows in chunk_rows:
        acc[rows, :] = mm(counts[rows, mesh_rows : 2 * mesh_rows], state[...])
    for copy in halo:
        copy.wait_recv()
    wide = []
    for rows in chunk_rows:
        own[1, rows, :] = (
            acc[rows, :]
            + mm(counts[rows, :mesh_rows], before_halo[...])
            + mm(counts[rows, 2 * mesh_rows :], after_halo[...])
        ).astype(jnp.bfloat16)
        wide.append(widen(1, rows))
    mesh_block(1, wide, pin_ref, pout_ref, state, final, lambda rows: None)

    back_out[...] = mm(placer[...], final[...], FIRST).astype(jnp.bfloat16)
    slots = []
    for k, offset in enumerate(slot_offsets):
        rows = pl.ds(k * cap, cap)
        slots.append(send(back_out.at[rows], back_in.at[rows], at(-offset)))
    grid_sum = mm(local_t[...], final[...])
    for copy in slots:
        copy.wait_recv()
    gown[...] = (grid_sum + mm(picker_t[...], back_in[...])).astype(jnp.bfloat16)
    send(gown, gother, peer).wait_recv()
    normed_a, normed_b, before = hidden_units(gown[...], gother[...], din_ref)
    gate = jax.nn.sigmoid(before)
    activated = (before * gate).astype(jnp.bfloat16)

    def put(row, values):
        rows = pl.ds(row, values.shape[0])
        grads[rows, :] = values
        stage[rows, :] = values.astype(jnp.bfloat16)

    blocks = half // LANES
    for side, cot in ((mp, cot_ref), (1 - mp, cot_other)):
        down = mm(activated, cot[...], FIRST)
        for b in range(blocks):
            row = pl.multiple_of((side * blocks + b) * hidden, hidden)
            put(row, down[:, b * LANES : (b + 1) * LANES])

    grid_sums = []

    def reduce_grid(i):
        copies = []
        for d in range(1, grid_n):
            to = lax.rem(mx + d, grid_n)
            rows = pl.ds(pl.multiple_of(i * piece + to * by_grid, by_grid), by_grid)
            copies.append(send(stage.at[rows], rx.at[i, d - 1], along("grid", mx, grid_n, d)))
        grid_sums.append(copies)

    ready = pieces // 2
    for i in range(ready):
        reduce_grid(i)

    before_grad = (hidden_grad[...] * gate * (1.0 + before * (1.0 - gate))).astype(jnp.bfloat16)
    for side, normed in ((mp, normed_a), (1 - mp, normed_b)):
        up = mm(normed, before_grad, FIRST)
        for b in range(hidden // LANES):
            row = pl.multiple_of(total // 2 + b * width + side * half, half)
            put(row, up[:, b * LANES : (b + 1) * LANES])
    for i in range(ready, pieces):
        reduce_grid(i)

    gpart_out[...] = mm(activated, dout_ref[:, second]).astype(jnp.bfloat16)
    decoded = send(gpart_out, gpart_in, peer)
    gkeep = mm(activated, dout_ref[:, first]) + grid_ref[...].astype(jnp.float32)

    mesh_sums = []
    for i in range(pieces):
        mine = pl.ds(pl.multiple_of(i * piece + mx * by_grid, by_grid), by_grid)
        value = grads[mine, :]
        for d, copy in enumerate(grid_sums[i]):
            copy.wait_recv()
            value = value + rx[i, d].astype(jnp.float32)
        acc_x[i] = value
        stage_z[i] = value.astype(jnp.bfloat16)
        copies = []
        for d in range(1, mesh_n):
            to = lax.rem(mz + d, mesh_n)
            rows = pl.ds(pl.multiple_of(to * by_mesh, by_mesh), by_mesh)
            copies.append(send(stage_z.at[i, rows], rz.at[i, d - 1], along("mesh", mz, mesh_n, d)))
        mesh_sums.append(copies)

    decoded.wait_recv()
    pred_ref[...] = (gkeep + gpart_in[...].astype(jnp.float32)).astype(jnp.bfloat16)

    spread_mesh = []
    for i in range(pieces):
        value = acc_x[i, pl.ds(pl.multiple_of(mz * by_mesh, by_mesh), by_mesh), :]
        for d, copy in enumerate(mesh_sums[i]):
            copy.wait_recv()
            value = value + rz[i, d].astype(jnp.float32)
        start = i * piece + mx * by_grid + mz * by_mesh
        rows = pl.ds(pl.multiple_of(start, by_mesh), by_mesh)
        red_ref[rows, :] = value.astype(jnp.bfloat16)
        spread_mesh.append(
            [
                send(red_ref.at[rows], red_ref.at[rows], along("mesh", mz, mesh_n, d))
                for d in range(1, mesh_n)
            ]
        )
    spread_grid = []
    for i in range(pieces):
        for copy in spread_mesh[i]:
            copy.wait_recv()
        rows = pl.ds(pl.multiple_of(i * piece + mx * by_grid, by_grid), by_grid)
        spread_grid += [
            send(red_ref.at[rows], red_ref.at[rows], along("grid", mx, grid_n, d))
            for d in range(1, grid_n)
        ]
    for copy in spread_grid:
        copy.wait_recv()
    for copy in started:
        copy.wait_send()


def on_device(sizes, *args):
    mesh_n, grid_n = sizes
    grid_latent, mesh_latent, local_targets, grid_slots, mesh_slots, mesh_links = args[:6]
    weights, cotangent = (args[6:12], args[12])
    grid_rows, half = grid_latent.shape
    mesh_rows = mesh_latent.shape[0]
    width, hidden = weights[0].shape
    cap4 = grid_slots.size
    total, pieces, piece, by_grid, by_mesh = plan(mesh_n, grid_n, width, hidden)
    copies = 4 + 1 + 4 + 4 + 4 + 4 + 1 + 1 + 2 * pieces * (grid_n - 1 + mesh_n - 1)
    bf16, f32 = (jnp.bfloat16, jnp.float32)
    scratch = [
        ((mesh_rows, 3 * mesh_rows), bf16),
        ((grid_rows, mesh_rows), bf16),
        ((grid_rows, cap4), bf16),
        ((mesh_rows, cap4), bf16),
        ((cap4, half), bf16),
        ((cap4, half), bf16),
        ((cap4, half), bf16),
        ((cap4, half), bf16),
        ((mesh_rows, half), f32),
        ((2, mesh_rows, half), bf16),
        ((2, mesh_rows, half), bf16),
        ((2, mesh_rows, half), bf16),
        ((2, mesh_rows, half), bf16),
        ((mesh_rows, half), f32),
        ((mesh_rows, half), bf16),
        ((mesh_rows, half), bf16),
        ((mesh_rows, half), bf16),
        ((mesh_rows, half), bf16),
        ((grid_rows, half), bf16),
        ((grid_rows, half), bf16),
        ((grid_rows, half), bf16),
        ((grid_rows, half), bf16),
        ((grid_rows, half), bf16),
        ((grid_rows, hidden), f32),
        ((total, LANES), f32),
        ((total, LANES), bf16),
        ((pieces, grid_n - 1, by_grid, LANES), bf16),
        ((pieces, by_grid, LANES), f32),
        ((pieces, by_grid, LANES), bf16),
        ((pieces, mesh_n - 1, by_mesh, LANES), bf16),
    ]
    vmem = pl.BlockSpec(memory_space=pltpu.VMEM)
    prediction, reduced = pl.pallas_call(
        functools.partial(kernel, sizes),
        out_shape=(
            jax.ShapeDtypeStruct((grid_rows, half), bf16),
            jax.ShapeDtypeStruct((total, LANES), bf16),
        ),
        in_specs=[vmem] * 13,
        out_specs=(vmem, vmem),
        scratch_shapes=[pltpu.VMEM(shape, dtype) for shape, dtype in scratch]
        + [pltpu.SemaphoreType.DMA((copies,)), pltpu.SemaphoreType.DMA((copies,))],
        compiler_params=pltpu.CompilerParams(
            collective_id=0, has_side_effects=True, vmem_limit_bytes=40 * 1024 * 1024
        ),
        name="forecast",
    )(
        grid_latent,
        mesh_latent,
        local_targets,
        grid_slots.reshape(1, cap4),
        mesh_slots.reshape(1, cap4),
        mesh_links,
        *weights,
        cotangent,
    )
    wide = reduced.astype(f32)
    down = wide[: total // 2].reshape(width // LANES, hidden, LANES)
    up = wide[total // 2 :].reshape(hidden // LANES, width, LANES)
    grad_down = jnp.concatenate([down[b] for b in range(down.shape[0])], axis=1)
    grad_up = jnp.concatenate([up[b] for b in range(up.shape[0])], axis=1)
    return (prediction, grad_up, grad_down)


def solution(mesh):
    sizes = (mesh.shape["mesh"], mesh.shape["grid"])
    rows = P(("groups", "mesh", "grid"), "mp")
    index = P(("mesh", "grid"), None)
    weights = (P(None, "mp"), P("mp", None)) * 3
    return jax.shard_map(
        functools.partial(on_device, sizes),
        mesh=mesh,
        in_specs=(rows, rows, index, index, index, index, *weights, rows),
        out_specs=(rows, P("groups", "mp"), P(("groups", "mp"), None)),
        check_vma=False,
    )
```

```python
import functools

import jax
import jax.numpy as jnp
from jax import lax
from jax.experimental import pallas as pl
from jax.experimental.pallas import tpu as pltpu
from jax.sharding import PartitionSpec as P

MESH = pl.DeviceIdType.MESH
slot_offsets = (-2, -1, 1, 2)
FIRST = (((0,), (0,)), ((), ()))
SECOND = (((1,), (1,)), ((), ()))
LANES = 128


def mm(a, b, dims=(((1,), (0,)), ((), ()))):
    return lax.dot_general(a, b, dims, preferred_element_type=jnp.float32)


def plan(mesh_axis, grid_axis, width, hidden):
    devices = mesh_axis * grid_axis
    total = 2 * width * hidden // LANES
    pieces = max(1, min(4, total // (16 * devices)))
    piece = total // pieces
    by_grid = piece // grid_axis
    return total, pieces, piece, by_grid, by_grid // mesh_axis


def kernel(
    sizes,
    grid_hbm,
    mesh_hbm,
    targets_hbm,
    gslots_hbm,
    mslots_hbm,
    links_hbm,
    ein_hbm,
    eout_hbm,
    pin_hbm,
    pout_hbm,
    din_hbm,
    dout_hbm,
    cot_hbm,
    pred_ref,
    red_ref,
    grid_ref,
    mesh_ref,
    targets_ref,
    gslots_ref,
    mslots_ref,
    links_ref,
    ein_ref,
    eout_ref,
    pin_ref,
    pout_ref,
    din_ref,
    dout_ref,
    cot_ref,
    links_col,
    targets_col,
    placer_rows,
    counts,
    local_t,
    picker_t,
    placer,
    out_slots,
    in_slots,
    back_out,
    back_in,
    acc,
    own,
    other,
    part_out,
    part_in,
    keep,
    state,
    halo,
    final,
    gown,
    gother,
    gpart_out,
    gpart_in,
    cot_other,
    hidden_grad,
    grads,
    stage,
    rx,
    acc_x,
    stage_z,
    rz,
    send_sems,
    recv_sems,
    load_sems,
):
    mesh_n, grid_n = sizes
    devices = mesh_n * grid_n
    grid_rows, half = grid_ref.shape
    mesh_rows = mesh_ref.shape[0]
    hidden = ein_ref.shape[1]
    width = ein_ref.shape[0]
    cap = gslots_ref.shape[1]
    total, pieces, piece, by_grid, by_mesh = plan(mesh_n, grid_n, width, hidden)
    loads = {}
    for name, src, dst in (
        ("grid", grid_hbm, grid_ref),
        ("gslots", gslots_hbm, gslots_ref),
        ("targets", targets_hbm, targets_ref),
        ("mslots", mslots_hbm, mslots_ref),
        ("cot", cot_hbm, cot_ref),
        ("ein", ein_hbm, ein_ref),
        ("eout", eout_hbm, eout_ref),
        ("mesh", mesh_hbm, mesh_ref),
        ("links", links_hbm, links_ref),
        ("dout", dout_hbm, dout_ref),
        ("pin", pin_hbm, pin_ref),
        ("pout", pout_hbm, pout_ref),
        ("din", din_hbm, din_ref),
    ):
        loads[name] = pltpu.make_async_copy(src, dst, load_sems.at[len(loads)])
        loads[name].start()

    def loaded(*wanted):
        for name in wanted:
            loads[name].wait()

    mz, mx, mp = (lax.axis_index("mesh"), lax.axis_index("grid"), lax.axis_index("mp"))
    place = mz * grid_n + mx
    peer = {"mp": 1 - mp}

    def at(offset):
        spot = lax.rem(place + (devices + offset), devices)
        return {"mesh": lax.div(spot, grid_n), "grid": lax.rem(spot, grid_n)}

    def along(axis, me, count, step):
        return {axis: lax.rem(me + step, count)}

    started = []

    def send(src, dst, device):
        index = len(started)
        copy = pltpu.make_async_remote_copy(
            src_ref=src,
            dst_ref=dst,
            send_sem=send_sems.at[index],
            recv_sem=recv_sems.at[index],
            device_id=device,
            device_id_type=MESH,
        )
        copy.start()
        started.append(copy)
        return copy

    partners = [peer] + [at(o) for o in slot_offsets]
    partners += [along("grid", mx, grid_n, d) for d in range(1, grid_n)]
    partners += [along("mesh", mz, mesh_n, d) for d in range(1, mesh_n)]
    barrier = pltpu.get_barrier_semaphore()
    for device in partners:
        pl.semaphore_signal(barrier, inc=1, device_id=device, device_id_type=MESH)

    rows_at = lambda n, m: lax.broadcasted_iota(jnp.int32, (n, m), 0)
    row_of = lambda ref: jnp.concatenate([ref[k : k + 1, :] for k in range(4)], axis=1)
    loaded("gslots")
    picker_t[...] = (
        (rows_at(grid_rows, 4 * cap) == row_of(gslots_ref)).astype(jnp.float32).astype(jnp.bfloat16)
    )
    loaded("grid")
    out_slots[...] = mm(picker_t[...], grid_ref[...], FIRST).astype(jnp.bfloat16)
    pl.semaphore_wait(barrier, len(partners))

    slots = []
    for k, offset in enumerate(slot_offsets):
        rows = pl.ds(k * cap, cap)
        slots.append(send(out_slots.at[rows], in_slots.at[rows], at(offset)))
    loaded("cot")
    cot_copy = send(cot_ref, cot_other, peer)
    loaded("mslots")
    placed = (rows_at(mesh_rows, 4 * cap) == row_of(mslots_ref)).astype(jnp.float32)
    placer[...] = placed.astype(jnp.bfloat16)

    def stand_up(ref):
        table = ref[...]
        missing = 8 - table.shape[0]
        table = jnp.concatenate([table, jnp.zeros((missing, table.shape[1]), jnp.int32)], axis=0)
        return jnp.transpose(table)

    def count_into(dst, src_ref, columns, start, rows, block):
        span = dst.shape[1]

        def body(i, carry):
            here = pl.ds(pl.multiple_of(start + i * block, block), block)
            window = lax.broadcasted_iota(jnp.int32, (block, span), 1)
            links = src_ref[here, :]
            found = jnp.zeros((block, span), jnp.float32)
            for k in range(columns):
                found = found + (links[:, k : k + 1] == window).astype(jnp.float32)
            dst[here, :] = found.astype(jnp.bfloat16)
            return carry

        lax.fori_loop(0, rows // block, body, 0)

    loaded("targets")
    targets_col[...] = stand_up(targets_ref)
    count_into(local_t, targets_col, targets_ref.shape[0], 0, grid_rows, 32)
    chunk = 256
    chunks = mesh_rows // chunk
    chunk_rows = [pl.ds(c * chunk, chunk) for c in range(chunks)]
    for rows in chunk_rows:
        acc[rows, :] = mm(local_t[:, rows], grid_ref[...], FIRST)

    first = pl.ds(pl.multiple_of(mp * half, half), half)
    second = pl.ds(pl.multiple_of((1 - mp) * half, half), half)

    def normalise(mine, theirs):
        a, b = (mine.astype(jnp.float32), theirs.astype(jnp.float32))
        mean = (jnp.sum(a, axis=1, keepdims=True) + jnp.sum(b, axis=1, keepdims=True)) / width
        a, b = (a - mean, b - mean)
        spread = jnp.sum(a * a, axis=1, keepdims=True) + jnp.sum(b * b, axis=1, keepdims=True)
        scale = lax.rsqrt(spread / width + 1e-05)
        return ((a * scale).astype(jnp.bfloat16), (b * scale).astype(jnp.bfloat16))

    def hidden_units(mine, theirs, in_ref):
        na, nb = normalise(mine, theirs)
        return (na, nb, mm(na, in_ref[first, :]) + mm(nb, in_ref[second, :]))

    def widen(which, rows):
        return send(own.at[which, rows], other.at[which, rows], peer)

    def mesh_block(which, wide, in_ref, out_ref, base_ref, dst_ref, after):
        parts = []
        for rows, copy in zip(chunk_rows, wide):
            copy.wait_recv()
            before = hidden_units(own[which, rows, :], other[which, rows, :], in_ref)[2]
            activated = (before * jax.nn.sigmoid(before)).astype(jnp.bfloat16)
            part_out[which, rows, :] = mm(activated, out_ref[:, second]).astype(jnp.bfloat16)
            parts.append(send(part_out.at[which, rows], part_in.at[which, rows], peer))
            keep[rows, :] = mm(activated, out_ref[:, first]) + base_ref[rows, :].astype(jnp.float32)
        for rows, copy in zip(chunk_rows, parts):
            copy.wait_recv()
            dst_ref[rows, :] = (
                keep[rows, :] + part_in[which, rows, :].astype(jnp.float32)
            ).astype(jnp.bfloat16)
            after(rows)

    for copy in slots:
        copy.wait_recv()
    wide = []
    for rows in chunk_rows:
        own[0, rows, :] = (mm(placer[rows, :], in_slots[...]) + acc[rows, :]).astype(jnp.bfloat16)
        wide.append(widen(0, rows))

    hop = 128
    arriving = []

    def send_halo(rows):
        for k in range(rows.size // hop):
            part = pl.ds(rows.start + k * hop, hop)
            if grid_n == 2:
                arriving.append(send(state.at[part], halo.at[mx, part], along("grid", mx, 2, 1)))
            else:
                arriving.append(send(state.at[part], halo.at[0, part], at(1)))
                arriving.append(send(state.at[part], halo.at[1, part], at(-1)))

    loaded("ein", "eout", "mesh")
    mesh_block(0, wide, ein_ref, eout_ref, mesh_ref, state, send_halo)

    loaded("links")
    links_col[...] = stand_up(links_ref)
    columns = links_ref.shape[0]
    steps = mesh_rows // hop

    def side_of(which):
        return pl.ds(pl.multiple_of(which * (2 * mesh_rows), mesh_rows), mesh_rows)

    def add_side(which):
        for rows in chunk_rows:
            acc[rows, :] = acc[rows, :] + mm(counts[rows, side_of(which)], halo[which])

    onward = []
    for k in range(steps):
        count_into(counts, links_col, columns, k * hop, hop, 32)
        if grid_n == 2:
            part = pl.ds(k * hop, hop)
            arriving[k].wait_recv()
            onward.append(send(halo.at[1 - mx, part], halo.at[mx, part], at(2 - 4 * mx)))
    for rows in chunk_rows:
        acc[rows, :] = mm(counts[rows, mesh_rows : 2 * mesh_rows], state[...])
    if grid_n == 2:
        add_side(1 - mx)
    cot_copy.wait_recv()
    loaded("dout")
    hidden_grad[...] = mm(cot_ref[...], dout_ref[:, first], SECOND) + mm(
        cot_other[...], dout_ref[:, second], SECOND
    )
    placer_rows[...] = jnp.transpose(placed).astype(jnp.bfloat16)
    if grid_n == 2:
        for copy in onward:
            copy.wait_recv()
        last = (mx,)
    else:
        for copy in arriving:
            copy.wait_recv()
        last = (0, 1)
    wide = []
    for rows in chunk_rows:
        own[1, rows, :] = (
            acc[rows, :] + sum(mm(counts[rows, side_of(which)], halo[which]) for which in last)
        ).astype(jnp.bfloat16)
        wide.append(widen(1, rows))
    loaded("pin", "pout", "din")
    mesh_block(1, wide, pin_ref, pout_ref, state, final, lambda rows: None)

    back_out[...] = mm(placer_rows[...], final[...]).astype(jnp.bfloat16)
    slots = []
    for k, offset in enumerate(slot_offsets):
        rows = pl.ds(k * cap, cap)
        slots.append(send(back_out.at[rows], back_in.at[rows], at(-offset)))
    grid_sum = mm(local_t[...], final[...])
    for copy in slots:
        copy.wait_recv()
    gown[...] = (grid_sum + mm(picker_t[...], back_in[...])).astype(jnp.bfloat16)
    send(gown, gother, peer).wait_recv()
    normed_a, normed_b, before = hidden_units(gown[...], gother[...], din_ref)
    gate = jax.nn.sigmoid(before)
    activated = (before * gate).astype(jnp.bfloat16)

    def put(row, values):
        rows = pl.ds(row, values.shape[0])
        grads[rows, :] = values
        stage[rows, :] = values.astype(jnp.bfloat16)

    blocks = half // LANES
    for side, cot in ((mp, cot_ref), (1 - mp, cot_other)):
        down = mm(activated, cot[...], FIRST)
        for b in range(blocks):
            row = pl.multiple_of((side * blocks + b) * hidden, hidden)
            put(row, down[:, b * LANES : (b + 1) * LANES])

    grid_sums = []

    def reduce_grid(i):
        copies = []
        for d in range(1, grid_n):
            to = lax.rem(mx + d, grid_n)
            rows = pl.ds(pl.multiple_of(i * piece + to * by_grid, by_grid), by_grid)
            copies.append(send(stage.at[rows], rx.at[i, d - 1], along("grid", mx, grid_n, d)))
        grid_sums.append(copies)

    ready = pieces // 2
    for i in range(ready):
        reduce_grid(i)

    before_grad = (hidden_grad[...] * gate * (1.0 + before * (1.0 - gate))).astype(jnp.bfloat16)
    for side, normed in ((mp, normed_a), (1 - mp, normed_b)):
        up = mm(normed, before_grad, FIRST)
        for b in range(hidden // LANES):
            row = pl.multiple_of(total // 2 + b * width + side * half, half)
            put(row, up[:, b * LANES : (b + 1) * LANES])
    for i in range(ready, pieces):
        reduce_grid(i)

    gpart_out[...] = mm(activated, dout_ref[:, second]).astype(jnp.bfloat16)
    decoded = send(gpart_out, gpart_in, peer)
    gkeep = mm(activated, dout_ref[:, first]) + grid_ref[...].astype(jnp.float32)

    mesh_sums = []
    for i in range(pieces):
        mine = pl.ds(pl.multiple_of(i * piece + mx * by_grid, by_grid), by_grid)
        value = grads[mine, :]
        for d, copy in enumerate(grid_sums[i]):
            copy.wait_recv()
            value = value + rx[i, d].astype(jnp.float32)
        acc_x[i] = value
        stage_z[i] = value.astype(jnp.bfloat16)
        copies = []
        for d in range(1, mesh_n):
            to = lax.rem(mz + d, mesh_n)
            rows = pl.ds(pl.multiple_of(to * by_mesh, by_mesh), by_mesh)
            copies.append(send(stage_z.at[i, rows], rz.at[i, d - 1], along("mesh", mz, mesh_n, d)))
        mesh_sums.append(copies)

    decoded.wait_recv()
    pred_ref[...] = (gkeep + gpart_in[...].astype(jnp.float32)).astype(jnp.bfloat16)

    spread_mesh = []
    for i in range(pieces):
        value = acc_x[i, pl.ds(pl.multiple_of(mz * by_mesh, by_mesh), by_mesh), :]
        for d, copy in enumerate(mesh_sums[i]):
            copy.wait_recv()
            value = value + rz[i, d].astype(jnp.float32)
        start = i * piece + mx * by_grid + mz * by_mesh
        rows = pl.ds(pl.multiple_of(start, by_mesh), by_mesh)
        red_ref[rows, :] = value.astype(jnp.bfloat16)
        spread_mesh.append(
            [
                send(red_ref.at[rows], red_ref.at[rows], along("mesh", mz, mesh_n, d))
                for d in range(1, mesh_n)
            ]
        )
    spread_grid = []
    for i in range(pieces):
        for copy in spread_mesh[i]:
            copy.wait_recv()
        rows = pl.ds(pl.multiple_of(i * piece + mx * by_grid, by_grid), by_grid)
        spread_grid += [
            send(red_ref.at[rows], red_ref.at[rows], along("grid", mx, grid_n, d))
            for d in range(1, grid_n)
        ]
    for copy in spread_grid:
        copy.wait_recv()
    for copy in started:
        copy.wait_send()


def on_device(sizes, *args):
    mesh_n, grid_n = sizes
    grid_latent, mesh_latent, local_targets, grid_slots, mesh_slots, mesh_links = args[:6]
    weights, cotangent = (args[6:12], args[12])
    grid_rows, half = grid_latent.shape
    mesh_rows = mesh_latent.shape[0]
    width, hidden = weights[0].shape
    cap4 = grid_slots.size
    total, pieces, piece, by_grid, by_mesh = plan(mesh_n, grid_n, width, hidden)
    copies = 4 + 1 + 4 + 4 + 4 * mesh_rows // 128 + 4 + 1 + 1 + 2 * pieces * (grid_n - 1 + mesh_n - 1)
    bf16, f32 = (jnp.bfloat16, jnp.float32)
    operands = (
        grid_latent,
        mesh_latent,
        local_targets.T,
        grid_slots,
        mesh_slots,
        mesh_links.T,
        *weights,
        cotangent,
    )
    scratch = [(x.shape, x.dtype) for x in operands] + [
        ((mesh_rows, 8), jnp.int32),
        ((grid_rows, 8), jnp.int32),
        ((cap4, mesh_rows), bf16),
        ((mesh_rows, 3 * mesh_rows), bf16),
        ((grid_rows, mesh_rows), bf16),
        ((grid_rows, cap4), bf16),
        ((mesh_rows, cap4), bf16),
        ((cap4, half), bf16),
        ((cap4, half), bf16),
        ((cap4, half), bf16),
        ((cap4, half), bf16),
        ((mesh_rows, half), f32),
        ((2, mesh_rows, half), bf16),
        ((2, mesh_rows, half), bf16),
        ((2, mesh_rows, half), bf16),
        ((2, mesh_rows, half), bf16),
        ((mesh_rows, half), f32),
        ((mesh_rows, half), bf16),
        ((2, mesh_rows, half), bf16),
        ((mesh_rows, half), bf16),
        ((grid_rows, half), bf16),
        ((grid_rows, half), bf16),
        ((grid_rows, half), bf16),
        ((grid_rows, half), bf16),
        ((grid_rows, half), bf16),
        ((grid_rows, hidden), f32),
        ((total, LANES), f32),
        ((total, LANES), bf16),
        ((pieces, grid_n - 1, by_grid, LANES), bf16),
        ((pieces, by_grid, LANES), f32),
        ((pieces, by_grid, LANES), bf16),
        ((pieces, mesh_n - 1, by_mesh, LANES), bf16),
    ]
    vmem = pl.BlockSpec(memory_space=pltpu.VMEM)
    prediction, reduced = pl.pallas_call(
        functools.partial(kernel, sizes),
        out_shape=(
            jax.ShapeDtypeStruct((grid_rows, half), bf16),
            jax.ShapeDtypeStruct((total, LANES), bf16),
        ),
        in_specs=[pl.BlockSpec(memory_space=pltpu.HBM)] * len(operands),
        out_specs=(vmem, vmem),
        scratch_shapes=[pltpu.VMEM(shape, dtype) for shape, dtype in scratch]
        + [pltpu.SemaphoreType.DMA((n,)) for n in (copies, copies, len(operands))],
        compiler_params=pltpu.CompilerParams(
            collective_id=0, has_side_effects=True, vmem_limit_bytes=40 * 1024 * 1024
        ),
        name="forecast",
    )(*operands)
    wide = reduced.astype(f32)
    down = wide[: total // 2].reshape(width // LANES, hidden, LANES)
    up = wide[total // 2 :].reshape(hidden // LANES, width, LANES)
    grad_down = jnp.concatenate([down[b] for b in range(down.shape[0])], axis=1)
    grad_up = jnp.concatenate([up[b] for b in range(up.shape[0])], axis=1)
    return (prediction, grad_up, grad_down)


def solution(mesh):
    sizes = (mesh.shape["mesh"], mesh.shape["grid"])
    rows = P(("groups", "mesh", "grid"), "mp")
    index = P(("mesh", "grid"), None)
    weights = (P(None, "mp"), P("mp", None)) * 3
    return jax.shard_map(
        functools.partial(on_device, sizes),
        mesh=mesh,
        in_specs=(rows, rows, index, index, index, index, *weights, rows),
        out_specs=(rows, P("groups", "mp"), P(("groups", "mp"), None)),
        check_vma=False,
    )
```

```python
import functools

import jax
import jax.numpy as jnp
from jax import lax
from jax.experimental import pallas as pl
from jax.experimental.pallas import tpu as pltpu
from jax.sharding import PartitionSpec as P

MESH = pl.DeviceIdType.MESH
slot_offsets = (-2, -1, 1, 2)
FIRST = (((0,), (0,)), ((), ()))
SECOND = (((1,), (1,)), ((), ()))
LANES = 128


def mm(a, b, dims=(((1,), (0,)), ((), ()))):
    return lax.dot_general(a, b, dims, preferred_element_type=jnp.float32)


def plan(mesh_axis, grid_axis, width, hidden):
    devices = mesh_axis * grid_axis
    total = 2 * width * hidden // LANES
    pieces = max(1, min(4, total // (16 * devices)))
    piece = total // pieces
    by_grid = piece // grid_axis
    return total, pieces, piece, by_grid, by_grid // mesh_axis


def kernel(
    sizes,
    grid_hbm,
    mesh_hbm,
    targets_hbm,
    gslots_hbm,
    mslots_hbm,
    links_hbm,
    ein_hbm,
    eout_hbm,
    pin_hbm,
    pout_hbm,
    din_hbm,
    dout_hbm,
    cot_hbm,
    pred_ref,
    red_ref,
    grid_ref,
    mesh_ref,
    targets_ref,
    gslots_ref,
    mslots_ref,
    links_ref,
    ein_ref,
    eout_ref,
    pin_ref,
    pout_ref,
    din_ref,
    dout_ref,
    cot_ref,
    links_col,
    targets_col,
    placer_rows,
    counts,
    local_t,
    picker_t,
    placer,
    out_slots,
    in_slots,
    back_out,
    back_in,
    acc,
    own,
    other,
    part_out,
    part_in,
    keep,
    state,
    halo,
    final,
    gown,
    gother,
    gpart_out,
    gpart_in,
    cot_other,
    hidden_grad,
    grads,
    stage,
    rx,
    acc_x,
    stage_z,
    rz,
    send_sems,
    recv_sems,
    load_sems,
):
    mesh_n, grid_n = sizes
    devices = mesh_n * grid_n
    grid_rows, half = grid_ref.shape
    mesh_rows = mesh_ref.shape[0]
    hidden = ein_ref.shape[1]
    width = ein_ref.shape[0]
    cap = gslots_ref.shape[1]
    total, pieces, piece, by_grid, by_mesh = plan(mesh_n, grid_n, width, hidden)
    loads = {}
    for name, src, dst in (
        ("gslots", gslots_hbm, gslots_ref),
        ("grid", grid_hbm, grid_ref),
        ("targets", targets_hbm, targets_ref),
        ("links", links_hbm, links_ref),
        ("mslots", mslots_hbm, mslots_ref),
        ("cot", cot_hbm, cot_ref),
        ("ein", ein_hbm, ein_ref),
        ("eout", eout_hbm, eout_ref),
        ("mesh", mesh_hbm, mesh_ref),
        ("dout", dout_hbm, dout_ref),
        ("pin", pin_hbm, pin_ref),
        ("pout", pout_hbm, pout_ref),
        ("din", din_hbm, din_ref),
    ):
        loads[name] = pltpu.make_async_copy(src, dst, load_sems.at[len(loads)])
        loads[name].start()

    def loaded(*wanted):
        for name in wanted:
            loads[name].wait()

    mz, mx, mp = (lax.axis_index("mesh"), lax.axis_index("grid"), lax.axis_index("mp"))
    place = mz * grid_n + mx
    peer = {"mp": 1 - mp}

    def at(offset):
        spot = lax.rem(place + (devices + offset), devices)
        return {"mesh": lax.div(spot, grid_n), "grid": lax.rem(spot, grid_n)}

    def along(axis, me, count, step):
        return {axis: lax.rem(me + step, count)}

    started = []

    def send(src, dst, device):
        index = len(started)
        copy = pltpu.make_async_remote_copy(
            src_ref=src,
            dst_ref=dst,
            send_sem=send_sems.at[index],
            recv_sem=recv_sems.at[index],
            device_id=device,
            device_id_type=MESH,
        )
        copy.start()
        started.append(copy)
        return copy

    partners = [peer] + [at(o) for o in slot_offsets]
    partners += [along("grid", mx, grid_n, d) for d in range(1, grid_n)]
    partners += [along("mesh", mz, mesh_n, d) for d in range(1, mesh_n)]
    barrier = pltpu.get_barrier_semaphore()
    for device in partners:
        pl.semaphore_signal(barrier, inc=1, device_id=device, device_id_type=MESH)

    rows_at = lambda n, m: lax.broadcasted_iota(jnp.int32, (n, m), 0)
    row_of = lambda ref: jnp.concatenate([ref[k : k + 1, :] for k in range(4)], axis=1)
    loaded("gslots")
    picker_t[...] = (
        (rows_at(grid_rows, 4 * cap) == row_of(gslots_ref)).astype(jnp.float32).astype(jnp.bfloat16)
    )
    loaded("grid")
    out_slots[...] = mm(picker_t[...], grid_ref[...], FIRST).astype(jnp.bfloat16)
    def stand_up(ref):
        table = ref[...]
        missing = 8 - table.shape[0]
        table = jnp.concatenate([table, jnp.zeros((missing, table.shape[1]), jnp.int32)], axis=0)
        return jnp.transpose(table)

    def count_into(dst, src_ref, columns, start, rows, block):
        span = dst.shape[1]

        def body(i, carry):
            here = pl.ds(pl.multiple_of(start + i * block, block), block)
            window = lax.broadcasted_iota(jnp.int32, (block, span), 1)
            links = src_ref[here, :]
            found = jnp.zeros((block, span), jnp.float32)
            for k in range(columns):
                found = found + (links[:, k : k + 1] == window).astype(jnp.float32)
            dst[here, :] = found.astype(jnp.bfloat16)
            return carry

        lax.fori_loop(0, rows // block, body, 0)

    pl.semaphore_wait(barrier, len(partners))

    slots = []
    for k, offset in enumerate(slot_offsets):
        rows = pl.ds(k * cap, cap)
        slots.append(send(out_slots.at[rows], in_slots.at[rows], at(offset)))
    loaded("cot")
    cot_copy = send(cot_ref, cot_other, peer)
    loaded("mslots")
    placed = (rows_at(mesh_rows, 4 * cap) == row_of(mslots_ref)).astype(jnp.float32)
    placer[...] = placed.astype(jnp.bfloat16)
    loaded("targets")
    targets_col[...] = stand_up(targets_ref)
    count_into(local_t, targets_col, targets_ref.shape[0], 0, grid_rows, 32)
    chunk = 256
    chunks = mesh_rows // chunk
    chunk_rows = [pl.ds(c * chunk, chunk) for c in range(chunks)]
    for rows in chunk_rows:
        acc[rows, :] = mm(local_t[:, rows], grid_ref[...], FIRST)

    loaded("links")
    links_col[...] = stand_up(links_ref)
    early = mesh_rows // 2
    count_into(counts, links_col, links_ref.shape[0], 0, early, 32)

    first = pl.ds(pl.multiple_of(mp * half, half), half)
    second = pl.ds(pl.multiple_of((1 - mp) * half, half), half)

    def normalise(mine, theirs):
        a, b = (mine.astype(jnp.float32), theirs.astype(jnp.float32))
        mean = (jnp.sum(a, axis=1, keepdims=True) + jnp.sum(b, axis=1, keepdims=True)) / width
        a, b = (a - mean, b - mean)
        spread = jnp.sum(a * a, axis=1, keepdims=True) + jnp.sum(b * b, axis=1, keepdims=True)
        scale = lax.rsqrt(spread / width + 1e-05)
        return ((a * scale).astype(jnp.bfloat16), (b * scale).astype(jnp.bfloat16))

    def hidden_units(mine, theirs, in_ref):
        na, nb = normalise(mine, theirs)
        return (na, nb, mm(na, in_ref[first, :]) + mm(nb, in_ref[second, :]))

    def widen(which, rows):
        return send(own.at[which, rows], other.at[which, rows], peer)

    def mesh_block(which, pieces_of, wide, in_ref, out_ref, base_ref, dst_ref, after):
        parts = []

        def complete(c):
            rows = pieces_of[c]
            parts[c].wait_recv()
            dst_ref[rows, :] = (
                keep[rows, :] + part_in[which, rows, :].astype(jnp.float32)
            ).astype(jnp.bfloat16)
            after(rows)

        for c, rows in enumerate(pieces_of):
            wide[c].wait_recv()
            before = hidden_units(own[which, rows, :], other[which, rows, :], in_ref)[2]
            activated = (before * jax.nn.sigmoid(before)).astype(jnp.bfloat16)
            part_out[which, rows, :] = mm(activated, out_ref[:, second]).astype(jnp.bfloat16)
            parts.append(send(part_out.at[which, rows], part_in.at[which, rows], peer))
            keep[rows, :] = mm(activated, out_ref[:, first]) + base_ref[rows, :].astype(jnp.float32)
            if c > 0:
                complete(c - 1)
        complete(len(pieces_of) - 1)

    for copy in slots:
        copy.wait_recv()
    hop = 128
    hop_rows = [pl.ds(c * hop, hop) for c in range(mesh_rows // hop)]
    wide = []
    for rows in hop_rows:
        own[0, rows, :] = (mm(placer[rows, :], in_slots[...]) + acc[rows, :]).astype(jnp.bfloat16)
        wide.append(widen(0, rows))

    arriving = []

    def send_halo(rows):
        for k in range(rows.size // hop):
            part = pl.ds(rows.start + k * hop, hop)
            if grid_n == 2:
                arriving.append(send(state.at[part], halo.at[mx, part], along("grid", mx, 2, 1)))
            else:
                arriving.append(send(state.at[part], halo.at[0, part], at(1)))
                arriving.append(send(state.at[part], halo.at[1, part], at(-1)))

    loaded("ein", "eout", "mesh")
    mesh_block(0, hop_rows, wide, ein_ref, eout_ref, mesh_ref, state, send_halo)

    count_into(counts, links_col, links_ref.shape[0], early, mesh_rows - early, 32)
    steps = mesh_rows // hop

    def side_of(which):
        return pl.ds(pl.multiple_of(which * (2 * mesh_rows), mesh_rows), mesh_rows)

    def add_side(which):
        for rows in chunk_rows:
            acc[rows, :] = acc[rows, :] + mm(counts[rows, side_of(which)], halo[which])

    onward = []
    for k in range(steps):
        if grid_n == 2:
            part = pl.ds(k * hop, hop)
            arriving[k].wait_recv()
            onward.append(send(halo.at[1 - mx, part], halo.at[mx, part], at(2 - 4 * mx)))
    for rows in chunk_rows:
        acc[rows, :] = mm(counts[rows, mesh_rows : 2 * mesh_rows], state[...])
    if grid_n == 2:
        add_side(1 - mx)
    cot_copy.wait_recv()
    loaded("dout")
    hidden_grad[...] = mm(cot_ref[...], dout_ref[:, first], SECOND) + mm(
        cot_other[...], dout_ref[:, second], SECOND
    )
    placer_rows[...] = jnp.transpose(placed).astype(jnp.bfloat16)
    if grid_n == 2:
        for copy in onward:
            copy.wait_recv()
        last = (mx,)
    else:
        for copy in arriving:
            copy.wait_recv()
        last = (0, 1)
    wide = []
    for rows in chunk_rows:
        own[1, rows, :] = (
            acc[rows, :] + sum(mm(counts[rows, side_of(which)], halo[which]) for which in last)
        ).astype(jnp.bfloat16)
        wide.append(widen(1, rows))
    loaded("pin", "pout", "din")
    mesh_block(1, chunk_rows, wide, pin_ref, pout_ref, state, final, lambda rows: None)

    back_out[...] = mm(placer_rows[...], final[...]).astype(jnp.bfloat16)
    slots = []
    for k, offset in enumerate(slot_offsets):
        rows = pl.ds(k * cap, cap)
        slots.append(send(back_out.at[rows], back_in.at[rows], at(-offset)))
    grid_sum = mm(local_t[...], final[...])
    for copy in slots:
        copy.wait_recv()
    gown[...] = (grid_sum + mm(picker_t[...], back_in[...])).astype(jnp.bfloat16)
    send(gown, gother, peer).wait_recv()
    normed_a, normed_b, before = hidden_units(gown[...], gother[...], din_ref)
    gate = jax.nn.sigmoid(before)
    activated = (before * gate).astype(jnp.bfloat16)

    def put(row, values):
        rows = pl.ds(row, values.shape[0])
        grads[rows, :] = values
        stage[rows, :] = values.astype(jnp.bfloat16)

    blocks = half // LANES
    activated_t = jnp.transpose(activated)
    for side, cot in ((mp, cot_ref), (1 - mp, cot_other)):
        down = mm(activated_t, cot[...])
        for b in range(blocks):
            row = pl.multiple_of((side * blocks + b) * hidden, hidden)
            put(row, down[:, b * LANES : (b + 1) * LANES])

    grid_sums = []

    def reduce_grid(i):
        copies = []
        for d in range(1, grid_n):
            to = lax.rem(mx + d, grid_n)
            rows = pl.ds(pl.multiple_of(i * piece + to * by_grid, by_grid), by_grid)
            copies.append(send(stage.at[rows], rx.at[i, d - 1], along("grid", mx, grid_n, d)))
        grid_sums.append(copies)

    ready = pieces // 2
    for i in range(ready):
        reduce_grid(i)

    before_grad = (hidden_grad[...] * gate * (1.0 + before * (1.0 - gate))).astype(jnp.bfloat16)
    for side, normed in ((mp, normed_a), (1 - mp, normed_b)):
        up = mm(normed, before_grad, FIRST)
        for b in range(hidden // LANES):
            row = pl.multiple_of(total // 2 + b * width + side * half, half)
            put(row, up[:, b * LANES : (b + 1) * LANES])
    for i in range(ready, pieces):
        reduce_grid(i)

    mesh_sums = []
    for i in range(pieces):
        mine = pl.ds(pl.multiple_of(i * piece + mx * by_grid, by_grid), by_grid)
        value = grads[mine, :]
        for d, copy in enumerate(grid_sums[i]):
            copy.wait_recv()
            value = value + rx[i, d].astype(jnp.float32)
        acc_x[i] = value
        stage_z[i] = value.astype(jnp.bfloat16)
        copies = []
        for d in range(1, mesh_n):
            to = lax.rem(mz + d, mesh_n)
            rows = pl.ds(pl.multiple_of(to * by_mesh, by_mesh), by_mesh)
            copies.append(send(stage_z.at[i, rows], rz.at[i, d - 1], along("mesh", mz, mesh_n, d)))
        mesh_sums.append(copies)

    gpart_out[...] = mm(activated, dout_ref[:, second]).astype(jnp.bfloat16)
    decoded = send(gpart_out, gpart_in, peer)
    gkeep = mm(activated, dout_ref[:, first]) + grid_ref[...].astype(jnp.float32)

    spread_mesh = []
    for i in range(pieces):
        value = acc_x[i, pl.ds(pl.multiple_of(mz * by_mesh, by_mesh), by_mesh), :]
        for d, copy in enumerate(mesh_sums[i]):
            copy.wait_recv()
            value = value + rz[i, d].astype(jnp.float32)
        start = i * piece + mx * by_grid + mz * by_mesh
        rows = pl.ds(pl.multiple_of(start, by_mesh), by_mesh)
        red_ref[rows, :] = value.astype(jnp.bfloat16)
        spread_mesh.append(
            [
                send(red_ref.at[rows], red_ref.at[rows], along("mesh", mz, mesh_n, d))
                for d in range(1, mesh_n)
            ]
        )
    decoded.wait_recv()
    pred_ref[...] = (gkeep + gpart_in[...].astype(jnp.float32)).astype(jnp.bfloat16)

    spread_grid = []
    for i in range(pieces):
        for copy in spread_mesh[i]:
            copy.wait_recv()
        rows = pl.ds(pl.multiple_of(i * piece + mx * by_grid, by_grid), by_grid)
        spread_grid += [
            send(red_ref.at[rows], red_ref.at[rows], along("grid", mx, grid_n, d))
            for d in range(1, grid_n)
        ]
    for copy in spread_grid:
        copy.wait_recv()
    for copy in started:
        copy.wait_send()


def finish(pred_in, red_in, pred_ref, up_ref, down_ref):
    pred_ref[...] = pred_in[...]
    hidden, width = down_ref.shape
    for b in range(width // LANES):
        down_ref[:, b * LANES : (b + 1) * LANES] = red_in[b * hidden : (b + 1) * hidden, :].astype(
            jnp.float32
        )
    start = width // LANES * hidden
    for b in range(hidden // LANES):
        rows = slice(start + b * width, start + (b + 1) * width)
        up_ref[:, b * LANES : (b + 1) * LANES] = red_in[rows, :].astype(jnp.float32)


def on_device(sizes, *args):
    mesh_n, grid_n = sizes
    grid_latent, mesh_latent, local_targets, grid_slots, mesh_slots, mesh_links = args[:6]
    weights, cotangent = (args[6:12], args[12])
    grid_rows, half = grid_latent.shape
    mesh_rows = mesh_latent.shape[0]
    width, hidden = weights[0].shape
    cap4 = grid_slots.size
    total, pieces, piece, by_grid, by_mesh = plan(mesh_n, grid_n, width, hidden)
    copies = 4 + 1 + 8 + 4 + 4 + 4 * mesh_rows // 128 + 4 + 1 + 1 + 2 * pieces * (grid_n - 1 + mesh_n - 1)
    bf16, f32 = (jnp.bfloat16, jnp.float32)
    operands = (
        grid_latent,
        mesh_latent,
        local_targets.T,
        grid_slots,
        mesh_slots,
        mesh_links.T,
        *weights,
        cotangent,
    )
    scratch = [(x.shape, x.dtype) for x in operands] + [
        ((mesh_rows, 8), jnp.int32),
        ((grid_rows, 8), jnp.int32),
        ((cap4, mesh_rows), bf16),
        ((mesh_rows, 3 * mesh_rows), bf16),
        ((grid_rows, mesh_rows), bf16),
        ((grid_rows, cap4), bf16),
        ((mesh_rows, cap4), bf16),
        ((cap4, half), bf16),
        ((cap4, half), bf16),
        ((cap4, half), bf16),
        ((cap4, half), bf16),
        ((mesh_rows, half), f32),
        ((2, mesh_rows, half), bf16),
        ((2, mesh_rows, half), bf16),
        ((2, mesh_rows, half), bf16),
        ((2, mesh_rows, half), bf16),
        ((mesh_rows, half), f32),
        ((mesh_rows, half), bf16),
        ((2, mesh_rows, half), bf16),
        ((mesh_rows, half), bf16),
        ((grid_rows, half), bf16),
        ((grid_rows, half), bf16),
        ((grid_rows, half), bf16),
        ((grid_rows, half), bf16),
        ((grid_rows, half), bf16),
        ((grid_rows, hidden), f32),
        ((total, LANES), f32),
        ((total, LANES), bf16),
        ((pieces, grid_n - 1, by_grid, LANES), bf16),
        ((pieces, by_grid, LANES), f32),
        ((pieces, by_grid, LANES), bf16),
        ((pieces, mesh_n - 1, by_mesh, LANES), bf16),
    ]
    vmem = pl.BlockSpec(memory_space=pltpu.VMEM)
    prediction, reduced = pl.pallas_call(
        functools.partial(kernel, sizes),
        out_shape=(
            jax.ShapeDtypeStruct((grid_rows, half), bf16),
            jax.ShapeDtypeStruct((total, LANES), bf16),
        ),
        in_specs=[pl.BlockSpec(memory_space=pltpu.HBM)] * len(operands),
        out_specs=(vmem, vmem),
        scratch_shapes=[pltpu.VMEM(shape, dtype) for shape, dtype in scratch]
        + [pltpu.SemaphoreType.DMA((n,)) for n in (copies, copies, len(operands))],
        compiler_params=pltpu.CompilerParams(
            collective_id=0, has_side_effects=True, vmem_limit_bytes=62 * 1024 * 1024
        ),
        name="forecast",
    )(*operands)
    return pl.pallas_call(
        finish,
        out_shape=(
            jax.ShapeDtypeStruct((grid_rows, half), bf16),
            jax.ShapeDtypeStruct((width, hidden), f32),
            jax.ShapeDtypeStruct((hidden, width), f32),
        ),
        in_specs=[vmem] * 2,
        out_specs=(vmem,) * 3,
        compiler_params=pltpu.CompilerParams(vmem_limit_bytes=62 * 1024 * 1024),
        name="widen_grads",
    )(prediction, reduced)


def solution(mesh):
    sizes = (mesh.shape["mesh"], mesh.shape["grid"])
    rows = P(("groups", "mesh", "grid"), "mp")
    index = P(("mesh", "grid"), None)
    weights = (P(None, "mp"), P("mp", None)) * 3
    return jax.shard_map(
        functools.partial(on_device, sizes),
        mesh=mesh,
        in_specs=(rows, rows, index, index, index, index, *weights, rows),
        out_specs=(rows, P("groups", "mp"), P(("groups", "mp"), None)),
        check_vma=False,
    )
```

```python
import functools

import jax
import jax.numpy as jnp
from jax import lax
from jax.experimental import pallas as pl
from jax.experimental.pallas import tpu as pltpu
from jax.sharding import PartitionSpec as P

MESH = pl.DeviceIdType.MESH
slot_offsets = (-2, -1, 1, 2)
FIRST = (((0,), (0,)), ((), ()))
SECOND = (((1,), (1,)), ((), ()))
LANES = 128


def mm(a, b, dims=(((1,), (0,)), ((), ()))):
    return lax.dot_general(a, b, dims, preferred_element_type=jnp.float32)


def plan(mesh_axis, grid_axis, width, hidden):
    devices = mesh_axis * grid_axis
    total = 2 * width * hidden // LANES
    pieces = max(1, min(4, total // (16 * devices)))
    piece = total // pieces
    by_grid = piece // grid_axis
    return total, pieces, piece, by_grid, by_grid // mesh_axis


def kernel(
    sizes,
    grid_hbm,
    mesh_hbm,
    targets_hbm,
    gslots_hbm,
    mslots_hbm,
    links_hbm,
    ein_hbm,
    eout_hbm,
    pin_hbm,
    pout_hbm,
    din_hbm,
    dout_hbm,
    cot_hbm,
    pred_ref,
    red_ref,
    grid_ref,
    mesh_ref,
    targets_ref,
    gslots_ref,
    mslots_ref,
    links_ref,
    ein_ref,
    eout_ref,
    pin_ref,
    pout_ref,
    din_ref,
    dout_ref,
    cot_ref,
    links_col,
    targets_col,
    placer_rows,
    counts,
    local_t,
    picker_t,
    placer,
    out_slots,
    in_slots,
    back_out,
    back_in,
    acc,
    own,
    other,
    part_out,
    part_in,
    keep,
    state,
    halo,
    final,
    gown,
    gother,
    gpart_out,
    gpart_in,
    cot_other,
    hidden_grad,
    grads,
    stage,
    rx,
    acc_x,
    stage_z,
    rz,
    send_sems,
    recv_sems,
    load_sems,
):
    mesh_n, grid_n = sizes
    devices = mesh_n * grid_n
    grid_rows, half = grid_ref.shape
    mesh_rows = mesh_ref.shape[0]
    hidden = ein_ref.shape[1]
    width = ein_ref.shape[0]
    cap = gslots_ref.shape[1]
    total, pieces, piece, by_grid, by_mesh = plan(mesh_n, grid_n, width, hidden)
    loads = {}
    for name, src, dst in (
        ("gslots", gslots_hbm, gslots_ref),
        ("grid", grid_hbm, grid_ref),
        ("targets", targets_hbm, targets_ref),
        ("links", links_hbm, links_ref),
        ("mslots", mslots_hbm, mslots_ref),
        ("cot", cot_hbm, cot_ref),
        ("ein", ein_hbm, ein_ref),
        ("eout", eout_hbm, eout_ref),
        ("mesh", mesh_hbm, mesh_ref),
        ("dout", dout_hbm, dout_ref),
        ("pin", pin_hbm, pin_ref),
        ("pout", pout_hbm, pout_ref),
        ("din", din_hbm, din_ref),
    ):
        loads[name] = pltpu.make_async_copy(src, dst, load_sems.at[len(loads)])
        loads[name].start()

    def loaded(*wanted):
        for name in wanted:
            loads[name].wait()

    mz, mx, mp = (lax.axis_index("mesh"), lax.axis_index("grid"), lax.axis_index("mp"))
    place = mz * grid_n + mx
    peer = {"mp": 1 - mp}

    def at(offset):
        spot = lax.rem(place + (devices + offset), devices)
        return {"mesh": lax.div(spot, grid_n), "grid": lax.rem(spot, grid_n)}

    def along(axis, me, count, step):
        return {axis: lax.rem(me + step, count)}

    started = []

    def send(src, dst, device):
        index = len(started)
        copy = pltpu.make_async_remote_copy(
            src_ref=src,
            dst_ref=dst,
            send_sem=send_sems.at[index],
            recv_sem=recv_sems.at[index],
            device_id=device,
            device_id_type=MESH,
        )
        copy.start()
        started.append(copy)
        return copy

    partners = [peer] + [at(o) for o in slot_offsets]
    partners += [along("grid", mx, grid_n, d) for d in range(1, grid_n)]
    partners += [along("mesh", mz, mesh_n, d) for d in range(1, mesh_n)]
    barrier = pltpu.get_barrier_semaphore()
    for device in partners:
        pl.semaphore_signal(barrier, inc=1, device_id=device, device_id_type=MESH)

    rows_at = lambda n, m: lax.broadcasted_iota(jnp.int32, (n, m), 0)
    row_of = lambda ref: jnp.concatenate([ref[k : k + 1, :] for k in range(4)], axis=1)
    loaded("gslots")
    picker_t[...] = (
        (rows_at(grid_rows, 4 * cap) == row_of(gslots_ref)).astype(jnp.float32).astype(jnp.bfloat16)
    )
    loaded("grid")
    out_slots[...] = mm(picker_t[...], grid_ref[...], FIRST).astype(jnp.bfloat16)
    def stand_up(ref):
        table = ref[...]
        missing = 8 - table.shape[0]
        table = jnp.concatenate([table, jnp.zeros((missing, table.shape[1]), jnp.int32)], axis=0)
        return jnp.transpose(table)

    def count_into(dst, src_ref, columns, start, rows, block):
        span = dst.shape[1]

        def body(i, carry):
            here = pl.ds(pl.multiple_of(start + i * block, block), block)
            window = lax.broadcasted_iota(jnp.int32, (block, span), 1)
            links = src_ref[here, :]
            found = jnp.zeros((block, span), jnp.float32)
            for k in range(columns):
                found = found + (links[:, k : k + 1] == window).astype(jnp.float32)
            dst[here, :] = found.astype(jnp.bfloat16)
            return carry

        lax.fori_loop(0, rows // block, body, 0)

    pl.semaphore_wait(barrier, len(partners))

    slots = []
    for k, offset in enumerate(slot_offsets):
        rows = pl.ds(k * cap, cap)
        slots.append(send(out_slots.at[rows], in_slots.at[rows], at(offset)))
    loaded("cot")
    cot_copy = send(cot_ref, cot_other, peer)
    loaded("mslots")
    placed = (rows_at(mesh_rows, 4 * cap) == row_of(mslots_ref)).astype(jnp.float32)
    placer[...] = placed.astype(jnp.bfloat16)
    loaded("targets")
    targets_col[...] = stand_up(targets_ref)
    count_into(local_t, targets_col, targets_ref.shape[0], 0, grid_rows, 32)
    chunk = 256
    chunks = mesh_rows // chunk
    chunk_rows = [pl.ds(c * chunk, chunk) for c in range(chunks)]
    for rows in chunk_rows:
        acc[rows, :] = mm(local_t[:, rows], grid_ref[...], FIRST)

    loaded("links")
    links_col[...] = stand_up(links_ref)
    count_into(counts, links_col, links_ref.shape[0], 0, mesh_rows, 32)

    first = pl.ds(pl.multiple_of(mp * half, half), half)
    second = pl.ds(pl.multiple_of((1 - mp) * half, half), half)

    def normalise(mine, theirs):
        a, b = (mine.astype(jnp.float32), theirs.astype(jnp.float32))
        mean = (jnp.sum(a, axis=1, keepdims=True) + jnp.sum(b, axis=1, keepdims=True)) / width
        a, b = (a - mean, b - mean)
        spread = jnp.sum(a * a, axis=1, keepdims=True) + jnp.sum(b * b, axis=1, keepdims=True)
        scale = lax.rsqrt(spread / width + 1e-05)
        return ((a * scale).astype(jnp.bfloat16), (b * scale).astype(jnp.bfloat16))

    def hidden_units(mine, theirs, in_ref):
        na, nb = normalise(mine, theirs)
        return (na, nb, mm(na, in_ref[first, :]) + mm(nb, in_ref[second, :]))

    def widen(which, rows):
        return send(own.at[which, rows], other.at[which, rows], peer)

    def mesh_block(which, pieces_of, wide, in_ref, out_ref, base_ref, dst_ref, after):
        parts = []

        def complete(c):
            rows = pieces_of[c]
            parts[c].wait_recv()
            dst_ref[rows, :] = (
                keep[rows, :] + part_in[which, rows, :].astype(jnp.float32)
            ).astype(jnp.bfloat16)
            after(rows)

        for c, rows in enumerate(pieces_of):
            wide[c].wait_recv()
            before = hidden_units(own[which, rows, :], other[which, rows, :], in_ref)[2]
            activated = (before * jax.nn.sigmoid(before)).astype(jnp.bfloat16)
            part_out[which, rows, :] = mm(activated, out_ref[:, second]).astype(jnp.bfloat16)
            parts.append(send(part_out.at[which, rows], part_in.at[which, rows], peer))
            keep[rows, :] = mm(activated, out_ref[:, first]) + base_ref[rows, :].astype(jnp.float32)
            if c > 0:
                complete(c - 1)
        complete(len(pieces_of) - 1)

    for copy in slots:
        copy.wait_recv()
    hop = 128
    hop_rows = [pl.ds(c * hop, hop) for c in range(mesh_rows // hop)]
    wide = []
    for rows in hop_rows:
        own[0, rows, :] = (mm(placer[rows, :], in_slots[...]) + acc[rows, :]).astype(jnp.bfloat16)
        wide.append(widen(0, rows))

    arriving = []

    def send_halo(rows):
        for k in range(rows.size // hop):
            part = pl.ds(rows.start + k * hop, hop)
            if grid_n == 2:
                arriving.append(send(state.at[part], halo.at[mx, part], along("grid", mx, 2, 1)))
            else:
                arriving.append(send(state.at[part], halo.at[0, part], at(1)))
                arriving.append(send(state.at[part], halo.at[1, part], at(-1)))

    loaded("ein", "eout", "mesh")
    mesh_block(0, hop_rows, wide, ein_ref, eout_ref, mesh_ref, state, send_halo)

    steps = mesh_rows // hop

    def side_of(which):
        return pl.ds(pl.multiple_of(which * (2 * mesh_rows), mesh_rows), mesh_rows)

    def add_side(which):
        for rows in chunk_rows:
            acc[rows, :] = acc[rows, :] + mm(counts[rows, side_of(which)], halo[which])

    onward = []
    for k in range(steps):
        if grid_n == 2:
            part = pl.ds(k * hop, hop)
            arriving[k].wait_recv()
            onward.append(send(halo.at[1 - mx, part], halo.at[mx, part], at(2 - 4 * mx)))
    for rows in chunk_rows:
        acc[rows, :] = mm(counts[rows, mesh_rows : 2 * mesh_rows], state[...])
    if grid_n == 2:
        add_side(1 - mx)
    cot_copy.wait_recv()
    loaded("dout")
    hidden_grad[...] = mm(cot_ref[...], dout_ref[:, first], SECOND) + mm(
        cot_other[...], dout_ref[:, second], SECOND
    )
    placer_rows[...] = jnp.transpose(placed).astype(jnp.bfloat16)
    if grid_n == 2:
        for copy in onward:
            copy.wait_recv()
        last = (mx,)
    else:
        for copy in arriving:
            copy.wait_recv()
        last = (0, 1)
    wide = []
    for rows in chunk_rows:
        own[1, rows, :] = (
            acc[rows, :] + sum(mm(counts[rows, side_of(which)], halo[which]) for which in last)
        ).astype(jnp.bfloat16)
        wide.append(widen(1, rows))
    loaded("pin", "pout", "din")
    mesh_block(1, chunk_rows, wide, pin_ref, pout_ref, state, final, lambda rows: None)

    back_out[...] = mm(placer_rows[...], final[...]).astype(jnp.bfloat16)
    slots = []
    for k, offset in enumerate(slot_offsets):
        rows = pl.ds(k * cap, cap)
        slots.append(send(back_out.at[rows], back_in.at[rows], at(-offset)))
    grid_sum = mm(local_t[...], final[...])
    for copy in slots:
        copy.wait_recv()
    gown[...] = (grid_sum + mm(picker_t[...], back_in[...])).astype(jnp.bfloat16)
    send(gown, gother, peer).wait_recv()
    normed_a, normed_b, before = hidden_units(gown[...], gother[...], din_ref)
    gate = jax.nn.sigmoid(before)
    activated = (before * gate).astype(jnp.bfloat16)

    def put(row, values):
        rows = pl.ds(row, values.shape[0])
        grads[rows, :] = values
        stage[rows, :] = values.astype(jnp.bfloat16)

    blocks = half // LANES
    activated_t = jnp.transpose(activated)
    for side, cot in ((mp, cot_ref), (1 - mp, cot_other)):
        down = mm(activated_t, cot[...])
        for b in range(blocks):
            row = pl.multiple_of((side * blocks + b) * hidden, hidden)
            put(row, down[:, b * LANES : (b + 1) * LANES])

    grid_sums = []

    def reduce_grid(i):
        copies = []
        for d in range(1, grid_n):
            to = lax.rem(mx + d, grid_n)
            rows = pl.ds(pl.multiple_of(i * piece + to * by_grid, by_grid), by_grid)
            copies.append(send(stage.at[rows], rx.at[i, d - 1], along("grid", mx, grid_n, d)))
        grid_sums.append(copies)

    ready = pieces // 2
    for i in range(ready):
        reduce_grid(i)

    before_grad = (hidden_grad[...] * gate * (1.0 + before * (1.0 - gate))).astype(jnp.bfloat16)
    for side, normed in ((mp, normed_a), (1 - mp, normed_b)):
        up = mm(normed, before_grad, FIRST)
        for b in range(hidden // LANES):
            row = pl.multiple_of(total // 2 + b * width + side * half, half)
            put(row, up[:, b * LANES : (b + 1) * LANES])
    for i in range(ready, pieces):
        reduce_grid(i)

    mesh_sums = []
    for i in range(pieces):
        mine = pl.ds(pl.multiple_of(i * piece + mx * by_grid, by_grid), by_grid)
        value = grads[mine, :]
        for d, copy in enumerate(grid_sums[i]):
            copy.wait_recv()
            value = value + rx[i, d].astype(jnp.float32)
        acc_x[i] = value
        stage_z[i] = value.astype(jnp.bfloat16)
        copies = []
        for d in range(1, mesh_n):
            to = lax.rem(mz + d, mesh_n)
            rows = pl.ds(pl.multiple_of(to * by_mesh, by_mesh), by_mesh)
            copies.append(send(stage_z.at[i, rows], rz.at[i, d - 1], along("mesh", mz, mesh_n, d)))
        mesh_sums.append(copies)

    gpart_out[...] = mm(activated, dout_ref[:, second]).astype(jnp.bfloat16)
    decoded = send(gpart_out, gpart_in, peer)
    gkeep = mm(activated, dout_ref[:, first]) + grid_ref[...].astype(jnp.float32)

    spread_mesh = []
    for i in range(pieces):
        value = acc_x[i, pl.ds(pl.multiple_of(mz * by_mesh, by_mesh), by_mesh), :]
        for d, copy in enumerate(mesh_sums[i]):
            copy.wait_recv()
            value = value + rz[i, d].astype(jnp.float32)
        start = i * piece + mx * by_grid + mz * by_mesh
        rows = pl.ds(pl.multiple_of(start, by_mesh), by_mesh)
        red_ref[rows, :] = value.astype(jnp.bfloat16)
        spread_mesh.append(
            [
                send(red_ref.at[rows], red_ref.at[rows], along("mesh", mz, mesh_n, d))
                for d in range(1, mesh_n)
            ]
        )
    decoded.wait_recv()
    pred_ref[...] = (gkeep + gpart_in[...].astype(jnp.float32)).astype(jnp.bfloat16)

    spread_grid = []
    for i in range(pieces):
        for copy in spread_mesh[i]:
            copy.wait_recv()
        rows = pl.ds(pl.multiple_of(i * piece + mx * by_grid, by_grid), by_grid)
        spread_grid += [
            send(red_ref.at[rows], red_ref.at[rows], along("grid", mx, grid_n, d))
            for d in range(1, grid_n)
        ]
    for copy in spread_grid:
        copy.wait_recv()
    for copy in started:
        copy.wait_send()


def finish(pred_in, red_in, pred_ref, up_ref, down_ref):
    pred_ref[...] = pred_in[...]
    hidden, width = down_ref.shape
    for b in range(width // LANES):
        down_ref[:, b * LANES : (b + 1) * LANES] = red_in[b * hidden : (b + 1) * hidden, :].astype(
            jnp.float32
        )
    start = width // LANES * hidden
    for b in range(hidden // LANES):
        rows = slice(start + b * width, start + (b + 1) * width)
        up_ref[:, b * LANES : (b + 1) * LANES] = red_in[rows, :].astype(jnp.float32)


def on_device(sizes, *args):
    mesh_n, grid_n = sizes
    grid_latent, mesh_latent, local_targets, grid_slots, mesh_slots, mesh_links = args[:6]
    weights, cotangent = (args[6:12], args[12])
    grid_rows, half = grid_latent.shape
    mesh_rows = mesh_latent.shape[0]
    width, hidden = weights[0].shape
    cap4 = grid_slots.size
    total, pieces, piece, by_grid, by_mesh = plan(mesh_n, grid_n, width, hidden)
    copies = 4 + 1 + 8 + 4 + 4 + 4 * mesh_rows // 128 + 4 + 1 + 1 + 2 * pieces * (grid_n - 1 + mesh_n - 1)
    bf16, f32 = (jnp.bfloat16, jnp.float32)
    operands = (
        grid_latent,
        mesh_latent,
        local_targets.T,
        grid_slots,
        mesh_slots,
        mesh_links.T,
        *weights,
        cotangent,
    )
    scratch = [(x.shape, x.dtype) for x in operands] + [
        ((mesh_rows, 8), jnp.int32),
        ((grid_rows, 8), jnp.int32),
        ((cap4, mesh_rows), bf16),
        ((mesh_rows, 3 * mesh_rows), bf16),
        ((grid_rows, mesh_rows), bf16),
        ((grid_rows, cap4), bf16),
        ((mesh_rows, cap4), bf16),
        ((cap4, half), bf16),
        ((cap4, half), bf16),
        ((cap4, half), bf16),
        ((cap4, half), bf16),
        ((mesh_rows, half), f32),
        ((2, mesh_rows, half), bf16),
        ((2, mesh_rows, half), bf16),
        ((2, mesh_rows, half), bf16),
        ((2, mesh_rows, half), bf16),
        ((mesh_rows, half), f32),
        ((mesh_rows, half), bf16),
        ((2, mesh_rows, half), bf16),
        ((mesh_rows, half), bf16),
        ((grid_rows, half), bf16),
        ((grid_rows, half), bf16),
        ((grid_rows, half), bf16),
        ((grid_rows, half), bf16),
        ((grid_rows, half), bf16),
        ((grid_rows, hidden), f32),
        ((total, LANES), f32),
        ((total, LANES), bf16),
        ((pieces, grid_n - 1, by_grid, LANES), bf16),
        ((pieces, by_grid, LANES), f32),
        ((pieces, by_grid, LANES), bf16),
        ((pieces, mesh_n - 1, by_mesh, LANES), bf16),
    ]
    vmem = pl.BlockSpec(memory_space=pltpu.VMEM)
    prediction, reduced = pl.pallas_call(
        functools.partial(kernel, sizes),
        out_shape=(
            jax.ShapeDtypeStruct((grid_rows, half), bf16),
            jax.ShapeDtypeStruct((total, LANES), bf16),
        ),
        in_specs=[pl.BlockSpec(memory_space=pltpu.HBM)] * len(operands),
        out_specs=(vmem, vmem),
        scratch_shapes=[pltpu.VMEM(shape, dtype) for shape, dtype in scratch]
        + [pltpu.SemaphoreType.DMA((n,)) for n in (copies, copies, len(operands))],
        compiler_params=pltpu.CompilerParams(
            collective_id=0, has_side_effects=True, vmem_limit_bytes=62 * 1024 * 1024
        ),
        name="forecast",
    )(*operands)
    return pl.pallas_call(
        finish,
        out_shape=(
            jax.ShapeDtypeStruct((grid_rows, half), bf16),
            jax.ShapeDtypeStruct((width, hidden), f32),
            jax.ShapeDtypeStruct((hidden, width), f32),
        ),
        in_specs=[vmem] * 2,
        out_specs=(vmem,) * 3,
        compiler_params=pltpu.CompilerParams(vmem_limit_bytes=62 * 1024 * 1024),
        name="widen_grads",
    )(prediction, reduced)


def solution(mesh):
    sizes = (mesh.shape["mesh"], mesh.shape["grid"])
    rows = P(("groups", "mesh", "grid"), "mp")
    index = P(("mesh", "grid"), None)
    weights = (P(None, "mp"), P("mp", None)) * 3
    return jax.shard_map(
        functools.partial(on_device, sizes),
        mesh=mesh,
        in_specs=(rows, rows, index, index, index, index, *weights, rows),
        out_specs=(rows, P("groups", "mp"), P(("groups", "mp"), None)),
        check_vma=False,
    )
```
